32 devices in a mesh: outer: 2 (over x), inner: 16 (over z, y, core).
Axes of the slice: x: 2, y: 2, z: 4, core: 2. Of those that a mesh axis runs over, the one named last changes fastest.
Arguments:
- queries: bfloat16 [4096, 2048], P('inner'), may hold values from -128 to 128
- mem_keys: bfloat16 [512, 2048], P(('outer', 'inner')), may hold values from -4.5 to 4.5
- mem_values: bfloat16 [512, 2048], P(('outer', 'inner')), may hold values from -6 to 6
Outputs:
- attended: bfloat16 [4096, 2048], P('inner')
- log_total: float32 [4096, 16], P('inner')
The draws below stay inside these ranges and needn't reach their ends.
All inputs are finite; a program needn't handle non-finite values.
Results may differ from the reference program's by a relative error of at most 0.014.
Values may be sent and summed in bfloat16 or wider, within the bound.
A program may use at most 64 MiB of HBM per device.

```python
import math
import jax
import jax.numpy as jnp
from jax import lax

HEADS = 16
HEAD_DIM = 128
TOKENS = 4096
MEMORY = 512
COLUMNS = 2048
N_OUTER = 2


def key_field(key):
    stream = jax.random.fold_in(key, 202)
    columns = HEADS * HEAD_DIM
    field = jnp.clip(jax.random.normal(stream, (MEMORY, columns), jnp.float32), -4.5, 4.5)
    return field.astype(jnp.bfloat16)


def draw_mem_keys(key, part):
    return key_field(key)


def draw_queries(key, part):
    stream = jax.random.fold_in(key, 303)
    columns = HEADS * HEAD_DIM
    field = 3.0 * jnp.clip(jax.random.normal(stream, (TOKENS, columns), jnp.float32), -6.0, 6.0)
    return field.astype(jnp.bfloat16)


def steps_of(stream_key, shape, cuts, low, high):
    def one(axis_at, parts):
        draws = jax.random.uniform(jax.random.fold_in(jax.random.fold_in(stream_key, 6), axis_at), (parts,), jnp.float32, low / len(cuts), high / len(cuts))
        return jnp.repeat(jnp.exp(draws), shape[axis_at] // parts).reshape((-1,) + (1,) * (len(shape) - axis_at - 1))

    factor_of = one(*cuts[0])
    for cut in cuts[1:]:
        factor_of = factor_of * one(*cut)
    return factor_of


def centred(key, shape, scale, bound, cuts=(), kind=jnp.bfloat16):
    entries = scale * jax.random.normal(key, shape, jnp.float32)
    if cuts:
        entries = entries * steps_of(key, shape, cuts, -0.22, 0.18)
    return jnp.clip(entries, -bound, bound).astype(kind)


def setup_inputs(seed: int = 0) -> dict:
    streams_of = jax.random.split(jax.random.key(seed), 4)
    return {
        "queries": draw_queries(jax.random.fold_in(streams_of[3], 71), 0),
        "mem_keys": draw_mem_keys(jax.random.fold_in(streams_of[3], 71), 0),
        "mem_values": centred(streams_of[2], (MEMORY, COLUMNS), 1.0, 6.0, ((0, 32),)),
    }


def reference(queries, mem_keys, mem_values):
    scale = 1.0 / math.sqrt(HEAD_DIM)
    per_group = MEMORY // N_OUTER
    key_groups = mem_keys.astype(jnp.float32).reshape(N_OUTER, per_group, HEADS, HEAD_DIM)
    value_groups = mem_values.astype(jnp.float32).reshape(N_OUTER, per_group, HEADS, HEAD_DIM)
    block_rows = math.gcd(TOKENS, 512)
    query_blocks = queries.astype(jnp.float32).reshape(TOKENS // block_rows, block_rows, HEADS, HEAD_DIM)

    def one_block(query_block):
        scores = jnp.einsum('thd,gkhd->thgk', query_block, key_groups) * scale
        group_peak = lax.optimization_barrier(jnp.max(scores, axis=-1))
        raw = jnp.exp(scores - group_peak[..., None])
        group_total = lax.optimization_barrier(jnp.sum(raw, axis=-1))
        weights = lax.optimization_barrier(raw.astype(jnp.bfloat16)).astype(jnp.float32)
        group_out = jnp.einsum('thgk,gkhd->thgd', weights, value_groups)
        peak = lax.optimization_barrier(jnp.max(group_peak, axis=-1))
        factor = jnp.exp(group_peak - peak[..., None])
        shares = lax.optimization_barrier((group_out * factor[..., None]).astype(jnp.bfloat16)).astype(jnp.float32)
        summed = lax.optimization_barrier(jnp.sum(shares, axis=2))
        total = lax.optimization_barrier(jnp.sum(group_total * factor, axis=-1))
        attended = (summed / total[..., None]).astype(jnp.bfloat16).reshape(block_rows, HEADS * HEAD_DIM)
        log_total = peak + jnp.log(total)
        return (attended, log_total)
    attended, log_total = lax.map(one_block, query_blocks)
    return (attended.reshape(TOKENS, HEADS * HEAD_DIM), log_total.reshape(TOKENS, HEADS))
```

```python
import functools
import math

import jax
import jax.numpy as jnp
from jax import lax
from jax.experimental import pallas as pl
from jax.experimental.pallas import tpu as pltpu
from jax.sharding import PartitionSpec as P

HEAD_DIM = 128
CHUNK_HEADS = 2
ENTRY_BLOCK = 512
MESH = pl.DeviceIdType.MESH


def attend(q, keys_of, values_of, entries):
    scale = 1.0 / math.sqrt(HEAD_DIM)
    to_two = scale * math.log2(math.e)
    block = math.gcd(entries, ENTRY_BLOCK)
    blocks = entries // block

    def scores_of(at):
        return lax.dot_general(
            keys_of(at, block), q, (((1,), (1,)), ((), ())), preferred_element_type=jnp.float32
        )

    def product_of(raw, at):
        return lax.dot_general(
            values_of(at, block),
            raw.astype(jnp.bfloat16),
            (((0,), (0,)), ((), ())),
            preferred_element_type=jnp.float32,
        )

    scores = scores_of(0)
    top = jnp.max(scores, axis=0, keepdims=True)
    raw = jnp.exp2((scores - top) * to_two)
    total = jnp.sum(raw, axis=0, keepdims=True)
    out = product_of(raw, 0)

    def step(number, running):
        top, total, out = running
        at = pl.multiple_of(number * block, block)
        scores = scores_of(at)
        new_top = jnp.maximum(top, jnp.max(scores, axis=0, keepdims=True))
        fading = jnp.exp2((top - new_top) * to_two)
        raw = jnp.exp2((scores - new_top) * to_two)
        total = total * fading + jnp.sum(raw, axis=0, keepdims=True)
        return new_top, total, out * fading + product_of(raw, at)

    if blocks > 1:
        top, total, out = lax.fori_loop(1, blocks, step, (top, total, out))
    return out / total, top * scale + jnp.log(total)


def kernel(
    n, Z, chunks, cw,
    q_hbm, k_ref, v_ref, out_ref, log_ref,
    qv, S, G, ob, lg,
    q_sem, x_send, x_recv, up_send, up_recv, dn_send, dn_recv,
    y_send, y_recv, c_send, c_recv, o_send, o_recv, own_sem, l_send, l_recv, l_own,
):
    o = lax.axis_index("outer")
    i = lax.axis_index("inner")
    c = lax.rem(i, 2)
    y = lax.rem(i // 2, 2)
    z = i // 4
    rows = k_ref.shape[0]
    R = rows * n
    row_of = Z * R
    lc = chunks * cw
    tokens = qv.shape[0]

    def inner_at(zz, yy, cc):
        return {"inner": (zz * 2 + yy) * 2 + cc}

    up, down = inner_at(z + 1, y, c), inner_at(z - 1, y, c)
    across, sibling = inner_at(z, 1 - y, c), inner_at(z, y, 1 - c)
    has_up, has_down = z < Z - 1, z > 0
    peers = [{"outer": lax.rem(o + d, n)} for d in range(1, n)]

    def row_start(yy, cc):
        return pl.multiple_of((cc * 2 + yy) * row_of, R)

    def block(k, zz):
        return G.at[k, pl.ds(pl.multiple_of(row_start(y, c) + zz * R, R), R), :]

    def copy(src, dst, send, recv, to):
        return pltpu.make_async_remote_copy(
            src_ref=src, dst_ref=dst, send_sem=send, recv_sem=recv, device_id=to, device_id_type=MESH
        )

    barrier = pltpu.get_barrier_semaphore()
    for to in peers + [across, sibling]:
        pl.semaphore_signal(barrier, inc=1, device_id=to, device_id_type=MESH)

    @pl.when(has_up)
    def _():
        pl.semaphore_signal(barrier, inc=1, device_id=up, device_id_type=MESH)

    @pl.when(has_down)
    def _():
        pl.semaphore_signal(barrier, inc=1, device_id=down, device_id_type=MESH)

    q_copy = pltpu.make_async_copy(
        q_hbm.at[:, pl.ds(pl.multiple_of(o * lc, 128), lc)], qv, q_sem
    )
    q_copy.start()
    for p in range(n):
        for k in range(chunks):
            at = p * lc + k * cw
            S[p, k, :, :cw] = k_ref[:, at : at + cw]
            S[p, k, :, cw:] = v_ref[:, at : at + cw]
    mine = pl.ds(pl.multiple_of(row_start(y, c) + z * R + o * rows, rows), rows)
    for k in range(chunks):
        G[k, mine, :] = S[o, k]

    pl.semaphore_wait(
        barrier, n + 1 + jnp.minimum(z, 1) + jnp.minimum(Z - 1 - z, 1)
    )

    for k in range(chunks):
        for to in peers:
            copy(S.at[to["outer"], k], G.at[k, mine, :], x_send.at[k], x_recv.at[k], to).start()

    def up_copy(k, s):
        b = block(k, z - s)
        return copy(b, b, up_send.at[k, s], up_recv.at[k, s], up)

    def down_copy(k, s):
        b = block(k, z + s)
        return copy(b, b, dn_send.at[k, s], dn_recv.at[k, s], down)

    def across_copy(k, zz):
        b = block(k, zz)
        return copy(b, b, y_send.at[k], y_recv.at[k], across)

    def line(k, yy, cc):
        return G.at[k, pl.ds(row_start(yy, cc), row_of), :]

    def sibling_copy(k, yy, which):
        b = line(k, yy, c)
        return copy(b, b, c_send.at[k, which], c_recv.at[k, which], sibling)

    def own(k):
        others = G.at[k, pl.ds(0, (n - 1) * rows), :]
        copy(others, others, x_send.at[k], x_recv.at[k], peers[0]).wait_recv()

        @pl.when(has_up)
        def _():
            up_copy(k, 0).start()

        @pl.when(has_down)
        def _():
            down_copy(k, 0).start()

        across_copy(k, z).start()

    def stage(k, s):
        @pl.when(z - s >= 0)
        def _():
            b = block(k, z - s)
            copy(b, b, up_send.at[k, s - 1], up_recv.at[k, s - 1], down).wait_recv()

            @pl.when(has_up)
            def _():
                up_copy(k, s).start()

            across_copy(k, z - s).start()

        @pl.when(z + s < Z)
        def _():
            b = block(k, z + s)
            copy(b, b, dn_send.at[k, s - 1], dn_recv.at[k, s - 1], up).wait_recv()

            @pl.when(has_down)
            def _():
                down_copy(k, s).start()

            across_copy(k, z + s).start()

        if s == Z - 1:
            sibling_copy(k, y, 0).start()

    def crossed(k):
        b = line(k, 1 - y, c)
        copy(b, b, y_send.at[k], y_recv.at[k], across).wait_recv()
        sibling_copy(k, 1 - y, 1).start()

    def out_at(k):
        return out_ref.at[:, pl.ds(pl.multiple_of(o * lc + k * cw, 128), cw)]

    def compute(k):
        if k == 0:
            q_copy.wait()
        for which, yy in ((0, y), (1, 1 - y)):
            b = line(k, yy, 1 - c)
            copy(b, b, c_send.at[k, which], c_recv.at[k, which], sibling).wait_recv()
        for h in range(cw // HEAD_DIM):
            lo = h * HEAD_DIM
            at = k * cw + lo
            out, log_total = attend(
                qv[:, at : at + HEAD_DIM],
                lambda e, size: G[k, pl.ds(e, size), lo : lo + HEAD_DIM],
                lambda e, size: G[k, pl.ds(e, size), cw + lo : cw + lo + HEAD_DIM],
                G.shape[1],
            )
            ob[k, :, lo : lo + HEAD_DIM] = out.T.astype(jnp.bfloat16)
            head = k * (cw // HEAD_DIM) + h
            lg[head : head + 1, :] = log_total
        for to in peers:
            copy(ob.at[k], out_at(k), o_send.at[k], o_recv.at[k], to).start()
        pltpu.make_async_copy(ob.at[k], out_at(k), own_sem.at[k]).start()

    events = []
    for k in range(chunks):
        events.append((3 * k, 0, k, functools.partial(own, k)))
        for s in range(1, Z):
            events.append((3 * k + 2 * s, 1, k, functools.partial(stage, k, s)))
        last = 3 * k + 2 * (Z - 1)
        events.append((last + 2, 2, k, functools.partial(crossed, k)))
        events.append((last + 3, 3, k, functools.partial(compute, k)))
    for event in sorted(events, key=lambda e: e[:3]):
        event[3]()

    log_copy = [copy(lg, log_ref.at[o], l_send, l_recv, to) for to in peers]
    for one in log_copy:
        one.start()
    log_own = pltpu.make_async_copy(lg, log_ref.at[o], l_own)
    log_own.start()

    for k in range(chunks):
        sent = G.at[k, pl.ds(0, (n - 1) * rows), :]
        copy(sent, sent, x_send.at[k], x_recv.at[k], peers[0]).wait_send()
        for s in range(Z - 1):
            @pl.when(jnp.logical_and(has_up, z - s >= 0))
            def _():
                up_copy(k, s).wait_send()

            @pl.when(jnp.logical_and(has_down, z + s < Z))
            def _():
                down_copy(k, s).wait_send()

        b = line(k, y, c)
        copy(b, b, y_send.at[k], y_recv.at[k], across).wait_send()
        sibling_copy(k, y, 0).wait_send()
        sibling_copy(k, 1 - y, 1).wait_send()
        pltpu.make_async_copy(ob.at[k], out_at(k), own_sem.at[k]).wait()
        some = out_ref.at[:, pl.ds(0, (n - 1) * cw)]
        whole = copy(some, some, o_send.at[k], o_recv.at[k], peers[0])
        whole.wait_send()
        whole.wait_recv()
    log_own.wait()
    some = log_ref.at[pl.ds(0, n - 1)]
    whole = copy(some, some, l_send, l_recv, peers[0])
    whole.wait_send()
    whole.wait_recv()


def on_device(n, inner, queries, mem_keys, mem_values):
    tokens, columns = queries.shape
    rows = mem_keys.shape[0]
    Z = inner // 4
    heads = columns // HEAD_DIM
    lh = heads // n
    lc = lh * HEAD_DIM
    cw = math.gcd(lh, CHUNK_HEADS) * HEAD_DIM
    chunks = lc // cw
    R = rows * n
    entries = inner * R
    dma = pltpu.SemaphoreType.DMA
    attended, logs = pl.pallas_call(
        functools.partial(kernel, n, Z, chunks, cw),
        out_shape=(
            jax.ShapeDtypeStruct((tokens, columns), jnp.bfloat16),
            jax.ShapeDtypeStruct((n, lh, tokens), jnp.float32),
        ),
        in_specs=[
            pl.BlockSpec(memory_space=pl.ANY),
            pl.BlockSpec(memory_space=pltpu.VMEM),
            pl.BlockSpec(memory_space=pltpu.VMEM),
        ],
        out_specs=(pl.BlockSpec(memory_space=pl.ANY), pl.BlockSpec(memory_space=pl.ANY)),
        scratch_shapes=[
            pltpu.VMEM((tokens, lc), jnp.bfloat16),
            pltpu.VMEM((n, chunks, rows, 2 * cw), jnp.bfloat16),
            pltpu.VMEM((chunks, entries, 2 * cw), jnp.bfloat16),
            pltpu.VMEM((chunks, tokens, cw), jnp.bfloat16),
            pltpu.VMEM((lh, tokens), jnp.float32),
            dma,
            dma((chunks,)), dma((chunks,)),
            dma((chunks, Z)), dma((chunks, Z)), dma((chunks, Z)), dma((chunks, Z)),
            dma((chunks,)), dma((chunks,)),
            dma((chunks, 2)), dma((chunks, 2)),
            dma((chunks,)), dma((chunks,)), dma((chunks,)),
            dma, dma, dma,
        ],
        compiler_params=pltpu.CompilerParams(
            collective_id=0, has_side_effects=True, vmem_limit_bytes=40 * 2**20
        ),
        cost_estimate=pl.CostEstimate(
            flops=4 * tokens * entries * lc,
            bytes_accessed=4 * tokens * columns,
            transcendentals=tokens * entries * lh,
        ),
    )(queries, mem_keys, mem_values)
    return attended, logs.reshape(heads, tokens).T


def solution(mesh):
    in_specs = (P("inner", None), P(("outer", "inner"), None), P(("outer", "inner"), None))
    out_specs = (P("inner", None), P("inner", None))
    return jax.shard_map(
        functools.partial(on_device, mesh.shape["outer"], mesh.shape["inner"]),
        mesh=mesh, in_specs=in_specs, out_specs=out_specs, check_vma=False,
    )
```

```python
import functools
import math

import jax
import jax.numpy as jnp
from jax import lax
from jax.experimental import pallas as pl
from jax.experimental.pallas import tpu as pltpu
from jax.sharding import PartitionSpec as P

HEAD_DIM = 128
CHUNK_HEADS = 2
CHUNK_STEP, STAGE_STEP = 1, 4
ENTRY_BLOCK = 512
MESH = pl.DeviceIdType.MESH


def attend(q, keys_of, values_of, entries):
    scale = 1.0 / math.sqrt(HEAD_DIM)
    to_two = scale * math.log2(math.e)
    block = math.gcd(entries, ENTRY_BLOCK)
    blocks = entries // block

    def scores_of(at):
        return lax.dot_general(
            keys_of(at, block), q, (((1,), (1,)), ((), ())), preferred_element_type=jnp.float32
        )

    def product_of(raw, at):
        return lax.dot_general(
            values_of(at, block),
            raw.astype(jnp.bfloat16),
            (((0,), (0,)), ((), ())),
            preferred_element_type=jnp.float32,
        )

    scores = scores_of(0)
    top = jnp.max(scores, axis=0, keepdims=True)
    raw = jnp.exp2((scores - top) * to_two)
    total = jnp.sum(raw, axis=0, keepdims=True)
    out = product_of(raw, 0)

    def step(number, running):
        top, total, out = running
        at = pl.multiple_of(number * block, block)
        scores = scores_of(at)
        new_top = jnp.maximum(top, jnp.max(scores, axis=0, keepdims=True))
        fading = jnp.exp2((top - new_top) * to_two)
        raw = jnp.exp2((scores - new_top) * to_two)
        total = total * fading + jnp.sum(raw, axis=0, keepdims=True)
        return new_top, total, out * fading + product_of(raw, at)

    if blocks > 1:
        top, total, out = lax.fori_loop(1, blocks, step, (top, total, out))
    return out / total, top * scale + jnp.log(total)


def kernel(
    n, Z, chunks, cw,
    q_hbm, k_hbm, v_hbm, out_ref, log_ref,
    k_ref, v_ref, k_sem, v_sem, qv, S, G, ob, lg,
    q_sem, x_send, x_recv, up_send, up_recv, dn_send, dn_recv,
    y_send, y_recv, c_send, c_recv, o_send, o_recv, own_sem, l_send, l_recv, l_own,
):
    o = lax.axis_index("outer")
    i = lax.axis_index("inner")
    c = lax.rem(i, 2)
    y = lax.rem(i // 2, 2)
    z = i // 4
    rows = k_ref.shape[0]
    R = rows * n
    row_of = Z * R
    lc = chunks * cw
    tokens = qv.shape[0]

    def inner_at(zz, yy, cc):
        return {"inner": (zz * 2 + yy) * 2 + cc}

    up, down = inner_at(z + 1, y, c), inner_at(z - 1, y, c)
    across, sibling = inner_at(z, 1 - y, c), inner_at(z, y, 1 - c)
    has_up, has_down = z < Z - 1, z > 0
    peers = [{"outer": lax.rem(o + d, n)} for d in range(1, n)]

    def row_start(yy, cc):
        return pl.multiple_of((cc * 2 + yy) * row_of, R)

    def block(k, zz):
        return G.at[k, pl.ds(pl.multiple_of(row_start(y, c) + zz * R, R), R), :]

    def copy(src, dst, send, recv, to):
        return pltpu.make_async_remote_copy(
            src_ref=src, dst_ref=dst, send_sem=send, recv_sem=recv, device_id=to, device_id_type=MESH
        )

    k_copy = pltpu.make_async_copy(k_hbm, k_ref, k_sem)
    v_copy = pltpu.make_async_copy(v_hbm, v_ref, v_sem)
    k_copy.start()
    v_copy.start()
    barrier = pltpu.get_barrier_semaphore()
    for to in peers + [across, sibling]:
        pl.semaphore_signal(barrier, inc=1, device_id=to, device_id_type=MESH)

    @pl.when(has_up)
    def _():
        pl.semaphore_signal(barrier, inc=1, device_id=up, device_id_type=MESH)

    @pl.when(has_down)
    def _():
        pl.semaphore_signal(barrier, inc=1, device_id=down, device_id_type=MESH)

    q_copy = pltpu.make_async_copy(
        q_hbm.at[:, pl.ds(pl.multiple_of(o * lc, 128), lc)], qv, q_sem
    )
    q_copy.start()
    k_copy.wait()
    v_copy.wait()
    for p in range(n):
        for k in range(chunks):
            at = p * lc + k * cw
            S[p, k, :, :cw] = k_ref[:, at : at + cw]
            S[p, k, :, cw:] = v_ref[:, at : at + cw]
    mine = pl.ds(pl.multiple_of(row_start(y, c) + z * R + o * rows, rows), rows)
    for k in range(chunks):
        G[k, mine, :] = S[o, k]

    pl.semaphore_wait(
        barrier, n + 1 + jnp.minimum(z, 1) + jnp.minimum(Z - 1 - z, 1)
    )

    for k in range(chunks):
        for to in peers:
            copy(S.at[to["outer"], k], G.at[k, mine, :], x_send.at[k], x_recv.at[k], to).start()

    def up_copy(k, s):
        b = block(k, z - s)
        return copy(b, b, up_send.at[k, s], up_recv.at[k, s], up)

    def down_copy(k, s):
        b = block(k, z + s)
        return copy(b, b, dn_send.at[k, s], dn_recv.at[k, s], down)

    def across_copy(k, zz):
        b = block(k, zz)
        return copy(b, b, y_send.at[k], y_recv.at[k], across)

    def line(k, yy, cc):
        return G.at[k, pl.ds(row_start(yy, cc), row_of), :]

    def sibling_copy(k, yy, which):
        b = line(k, yy, c)
        return copy(b, b, c_send.at[k, which], c_recv.at[k, which], sibling)

    def own(k):
        others = G.at[k, pl.ds(0, (n - 1) * rows), :]
        copy(others, others, x_send.at[k], x_recv.at[k], peers[0]).wait_recv()

        @pl.when(has_up)
        def _():
            up_copy(k, 0).start()

        @pl.when(has_down)
        def _():
            down_copy(k, 0).start()

        across_copy(k, z).start()

    def stage(k, s):
        @pl.when(z - s >= 0)
        def _():
            b = block(k, z - s)
            copy(b, b, up_send.at[k, s - 1], up_recv.at[k, s - 1], down).wait_recv()

            @pl.when(has_up)
            def _():
                up_copy(k, s).start()

            across_copy(k, z - s).start()

        @pl.when(z + s < Z)
        def _():
            b = block(k, z + s)
            copy(b, b, dn_send.at[k, s - 1], dn_recv.at[k, s - 1], up).wait_recv()

            @pl.when(has_down)
            def _():
                down_copy(k, s).start()

            across_copy(k, z + s).start()

        if s == Z - 1:
            sibling_copy(k, y, 0).start()

    def crossed(k):
        b = line(k, 1 - y, c)
        copy(b, b, y_send.at[k], y_recv.at[k], across).wait_recv()
        sibling_copy(k, 1 - y, 1).start()

    def out_at(k):
        return out_ref.at[:, pl.ds(pl.multiple_of(o * lc + k * cw, 128), cw)]

    def compute(k):
        if k == 0:
            q_copy.wait()
        for which, yy in ((0, y), (1, 1 - y)):
            b = line(k, yy, 1 - c)
            copy(b, b, c_send.at[k, which], c_recv.at[k, which], sibling).wait_recv()
        for h in range(cw // HEAD_DIM):
            lo = h * HEAD_DIM
            at = k * cw + lo
            out, log_total = attend(
                qv[:, at : at + HEAD_DIM],
                lambda e, size: G[k, pl.ds(e, size), lo : lo + HEAD_DIM],
                lambda e, size: G[k, pl.ds(e, size), cw + lo : cw + lo + HEAD_DIM],
                G.shape[1],
            )
            ob[k, :, lo : lo + HEAD_DIM] = out.T.astype(jnp.bfloat16)
            head = k * (cw // HEAD_DIM) + h
            lg[head : head + 1, :] = log_total
        for to in peers:
            copy(ob.at[k], out_at(k), o_send.at[k], o_recv.at[k], to).start()
        pltpu.make_async_copy(ob.at[k], out_at(k), own_sem.at[k]).start()

    events = []
    for k in range(chunks):
        events.append((CHUNK_STEP * k, 0, k, functools.partial(own, k)))
        for s in range(1, Z):
            events.append((CHUNK_STEP * k + STAGE_STEP * s, 1, k, functools.partial(stage, k, s)))
        last = CHUNK_STEP * k + STAGE_STEP * (Z - 1)
        events.append((last + 2, 2, k, functools.partial(crossed, k)))
        events.append((last + 3, 3, k, functools.partial(compute, k)))
    for event in sorted(events, key=lambda e: e[:3]):
        event[3]()

    log_copy = [copy(lg, log_ref.at[o], l_send, l_recv, to) for to in peers]
    for one in log_copy:
        one.start()
    log_own = pltpu.make_async_copy(lg, log_ref.at[o], l_own)
    log_own.start()

    for k in range(chunks):
        sent = G.at[k, pl.ds(0, (n - 1) * rows), :]
        copy(sent, sent, x_send.at[k], x_recv.at[k], peers[0]).wait_send()
        for s in range(Z - 1):
            @pl.when(jnp.logical_and(has_up, z - s >= 0))
            def _():
                up_copy(k, s).wait_send()

            @pl.when(jnp.logical_and(has_down, z + s < Z))
            def _():
                down_copy(k, s).wait_send()

        b = line(k, y, c)
        copy(b, b, y_send.at[k], y_recv.at[k], across).wait_send()
        sibling_copy(k, y, 0).wait_send()
        sibling_copy(k, 1 - y, 1).wait_send()
        pltpu.make_async_copy(ob.at[k], out_at(k), own_sem.at[k]).wait()
        some = out_ref.at[:, pl.ds(0, (n - 1) * cw)]
        whole = copy(some, some, o_send.at[k], o_recv.at[k], peers[0])
        whole.wait_send()
        whole.wait_recv()
    log_own.wait()
    some = log_ref.at[pl.ds(0, n - 1)]
    whole = copy(some, some, l_send, l_recv, peers[0])
    whole.wait_send()
    whole.wait_recv()


def on_device(n, inner, queries, mem_keys, mem_values):
    tokens, columns = queries.shape
    rows = mem_keys.shape[0]
    Z = inner // 4
    heads = columns // HEAD_DIM
    lh = heads // n
    lc = lh * HEAD_DIM
    cw = math.gcd(lh, CHUNK_HEADS) * HEAD_DIM
    chunks = lc // cw
    R = rows * n
    entries = inner * R
    dma = pltpu.SemaphoreType.DMA
    attended, logs = pl.pallas_call(
        functools.partial(kernel, n, Z, chunks, cw),
        out_shape=(
            jax.ShapeDtypeStruct((tokens, columns), jnp.bfloat16),
            jax.ShapeDtypeStruct((n, lh, tokens), jnp.float32),
        ),
        in_specs=[
            pl.BlockSpec(memory_space=pltpu.HBM),
            pl.BlockSpec(memory_space=pltpu.HBM),
            pl.BlockSpec(memory_space=pltpu.HBM),
        ],
        out_specs=(pl.BlockSpec(memory_space=pl.ANY), pl.BlockSpec(memory_space=pl.ANY)),
        scratch_shapes=[
            pltpu.VMEM(mem_keys.shape, jnp.bfloat16),
            pltpu.VMEM(mem_keys.shape, jnp.bfloat16),
            dma,
            dma,
            pltpu.VMEM((tokens, lc), jnp.bfloat16),
            pltpu.VMEM((n, chunks, rows, 2 * cw), jnp.bfloat16),
            pltpu.VMEM((chunks, entries, 2 * cw), jnp.bfloat16),
            pltpu.VMEM((chunks, tokens, cw), jnp.bfloat16),
            pltpu.VMEM((lh, tokens), jnp.float32),
            dma,
            dma((chunks,)), dma((chunks,)),
            dma((chunks, Z)), dma((chunks, Z)), dma((chunks, Z)), dma((chunks, Z)),
            dma((chunks,)), dma((chunks,)),
            dma((chunks, 2)), dma((chunks, 2)),
            dma((chunks,)), dma((chunks,)), dma((chunks,)),
            dma, dma, dma,
        ],
        compiler_params=pltpu.CompilerParams(
            collective_id=0, has_side_effects=True, vmem_limit_bytes=40 * 2**20
        ),
        cost_estimate=pl.CostEstimate(
            flops=4 * tokens * entries * lc,
            bytes_accessed=4 * tokens * columns,
            transcendentals=tokens * entries * lh,
        ),
    )(queries, mem_keys, mem_values)
    return attended, logs.reshape(heads, tokens).T


def solution(mesh):
    in_specs = (P("inner", None), P(("outer", "inner"), None), P(("outer", "inner"), None))
    out_specs = (P("inner", None), P("inner", None))
    return jax.shard_map(
        functools.partial(on_device, mesh.shape["outer"], mesh.shape["inner"]),
        mesh=mesh, in_specs=in_specs, out_specs=out_specs, check_vma=False,
    )
```

```python
import functools
import math

import jax
import jax.numpy as jnp
from jax import lax
from jax.experimental import pallas as pl
from jax.experimental.pallas import tpu as pltpu
from jax.sharding import PartitionSpec as P

HEAD_DIM = 128
CHUNK_HEADS = 2
CHUNK_STEP, STAGE_STEP = 1, 4
ENTRY_BLOCK = 512
MESH = pl.DeviceIdType.MESH


def attend(q, keys_of, values_of, entries):
    scale = 1.0 / math.sqrt(HEAD_DIM)
    to_two = scale * math.log2(math.e)
    block = math.gcd(entries, ENTRY_BLOCK)
    blocks = entries // block

    def scores_of(at):
        return lax.dot_general(
            keys_of(at, block), q, (((1,), (1,)), ((), ())), preferred_element_type=jnp.float32
        )

    def product_of(raw, at):
        return lax.dot_general(
            values_of(at, block),
            raw.astype(jnp.bfloat16),
            (((0,), (0,)), ((), ())),
            preferred_element_type=jnp.float32,
        )

    scores = scores_of(0)
    top = jnp.max(scores, axis=0, keepdims=True)
    raw = jnp.exp2((scores - top) * to_two)
    total = jnp.sum(raw, axis=0, keepdims=True)
    out = product_of(raw, 0)

    def step(number, running):
        top, total, out = running
        at = pl.multiple_of(number * block, block)
        scores = scores_of(at)
        new_top = jnp.maximum(top, jnp.max(scores, axis=0, keepdims=True))
        fading = jnp.exp2((top - new_top) * to_two)
        raw = jnp.exp2((scores - new_top) * to_two)
        total = total * fading + jnp.sum(raw, axis=0, keepdims=True)
        return new_top, total, out * fading + product_of(raw, at)

    if blocks > 1:
        top, total, out = lax.fori_loop(1, blocks, step, (top, total, out))
    return out / total, top * scale + jnp.log(total)


def kernel(
    n, Z, chunks, cw,
    q_hbm, k_hbm, v_hbm, out_ref, log_ref,
    k_ref, v_ref, k_sem, v_sem, qv, S, G, ob, lg,
    q_sem, x_send, x_recv, up_send, up_recv, dn_send, dn_recv,
    y_send, y_recv, c_send, c_recv, o_send, o_recv, own_sem, l_send, l_recv, l_own,
):
    o = lax.axis_index("outer")
    i = lax.axis_index("inner")
    c = lax.rem(i, 2)
    y = lax.rem(i // 2, 2)
    z = i // 4
    rows = k_ref.shape[0]
    R = rows * n
    row_of = Z * R
    lc = chunks * cw
    tokens = qv.shape[0]

    def inner_at(zz, yy, cc):
        return {"inner": (zz * 2 + yy) * 2 + cc}

    up, down = inner_at(z + 1, y, c), inner_at(z - 1, y, c)
    across, sibling = inner_at(z, 1 - y, c), inner_at(z, y, 1 - c)
    has_up, has_down = z < Z - 1, z > 0
    peers = [{"outer": lax.rem(o + d, n)} for d in range(1, n)]

    def row_start(yy, cc):
        return pl.multiple_of((cc * 2 + yy) * row_of, R)

    def block(k, zz):
        return G.at[k, pl.ds(pl.multiple_of(row_start(y, c) + zz * R, R), R), :]

    def copy(src, dst, send, recv, to):
        return pltpu.make_async_remote_copy(
            src_ref=src, dst_ref=dst, send_sem=send, recv_sem=recv, device_id=to, device_id_type=MESH
        )

    k_copy = pltpu.make_async_copy(k_hbm, k_ref, k_sem)
    v_copy = pltpu.make_async_copy(v_hbm, v_ref, v_sem)
    k_copy.start()
    v_copy.start()
    barrier = pltpu.get_barrier_semaphore()
    for to in peers + [across, sibling]:
        pl.semaphore_signal(barrier, inc=1, device_id=to, device_id_type=MESH)

    @pl.when(has_up)
    def _():
        pl.semaphore_signal(barrier, inc=1, device_id=up, device_id_type=MESH)

    @pl.when(has_down)
    def _():
        pl.semaphore_signal(barrier, inc=1, device_id=down, device_id_type=MESH)

    q_copy = pltpu.make_async_copy(
        q_hbm.at[:, pl.ds(pl.multiple_of(o * lc, 128), lc)], qv, q_sem
    )
    q_copy.start()
    k_copy.wait()
    v_copy.wait()
    for p in range(n):
        for k in range(chunks):
            at = p * lc + k * cw
            S[p, k, :, :cw] = k_ref[:, at : at + cw]
            S[p, k, :, cw:] = v_ref[:, at : at + cw]
    mine = pl.ds(pl.multiple_of(row_start(y, c) + z * R + o * rows, rows), rows)
    for k in range(chunks):
        G[k, mine, :] = S[o, k]

    pl.semaphore_wait(
        barrier, n + 1 + jnp.minimum(z, 1) + jnp.minimum(Z - 1 - z, 1)
    )

    for k in range(chunks):
        for to in peers:
            copy(S.at[to["outer"], k], G.at[k, mine, :], x_send.at[k], x_recv.at[k], to).start()

    def up_copy(k, s):
        b = block(k, z - s)
        return copy(b, b, up_send.at[k, s], up_recv.at[k, s], up)

    def down_copy(k, s):
        b = block(k, z + s)
        return copy(b, b, dn_send.at[k, s], dn_recv.at[k, s], down)

    def across_copy(k, zz):
        b = block(k, zz)
        return copy(b, b, y_send.at[k], y_recv.at[k], across)

    def line(k, yy, cc):
        return G.at[k, pl.ds(row_start(yy, cc), row_of), :]

    def sibling_copy(k, yy, which):
        b = line(k, yy, c)
        return copy(b, b, c_send.at[k, which], c_recv.at[k, which], sibling)

    def piece(k, d):
        at = row_start(y, c) + z * R + lax.rem(o + d, n) * rows
        return G.at[k, pl.ds(pl.multiple_of(at, rows), rows), :]

    def send_piece(k, d):
        b = piece(k, d)

        @pl.when(has_up)
        def _():
            copy(b, b, up_send.at[k, 0], up_recv.at[k, 0], up).start()

        @pl.when(has_down)
        def _():
            copy(b, b, dn_send.at[k, 0], dn_recv.at[k, 0], down).start()

        copy(b, b, y_send.at[k], y_recv.at[k], across).start()

    for k in range(chunks):
        send_piece(k, 0)

    def own(k):
        others = G.at[k, pl.ds(0, (n - 1) * rows), :]
        copy(others, others, x_send.at[k], x_recv.at[k], peers[0]).wait_recv()

        for d in range(1, n):
            send_piece(k, d)

    def stage(k, s):
        @pl.when(z - s >= 0)
        def _():
            b = block(k, z - s)
            copy(b, b, up_send.at[k, s - 1], up_recv.at[k, s - 1], down).wait_recv()

            @pl.when(has_up)
            def _():
                up_copy(k, s).start()

            across_copy(k, z - s).start()

        @pl.when(z + s < Z)
        def _():
            b = block(k, z + s)
            copy(b, b, dn_send.at[k, s - 1], dn_recv.at[k, s - 1], up).wait_recv()

            @pl.when(has_down)
            def _():
                down_copy(k, s).start()

            across_copy(k, z + s).start()

        if s == Z - 1:
            sibling_copy(k, y, 0).start()

    def crossed(k):
        b = line(k, 1 - y, c)
        copy(b, b, y_send.at[k], y_recv.at[k], across).wait_recv()
        sibling_copy(k, 1 - y, 1).start()

    def out_at(k):
        return out_ref.at[:, pl.ds(pl.multiple_of(o * lc + k * cw, 128), cw)]

    def compute(k):
        if k == 0:
            q_copy.wait()
        for which, yy in ((0, y), (1, 1 - y)):
            b = line(k, yy, 1 - c)
            copy(b, b, c_send.at[k, which], c_recv.at[k, which], sibling).wait_recv()
        for h in range(cw // HEAD_DIM):
            lo = h * HEAD_DIM
            at = k * cw + lo
            out, log_total = attend(
                qv[:, at : at + HEAD_DIM],
                lambda e, size: G[k, pl.ds(e, size), lo : lo + HEAD_DIM],
                lambda e, size: G[k, pl.ds(e, size), cw + lo : cw + lo + HEAD_DIM],
                G.shape[1],
            )
            ob[k, :, lo : lo + HEAD_DIM] = out.T.astype(jnp.bfloat16)
            head = k * (cw // HEAD_DIM) + h
            column = pl.multiple_of(o * lc + at, HEAD_DIM)
            place = out_ref.at[:, pl.ds(column, HEAD_DIM)]
            for to in peers:
                copy(ob.at[k, :, lo : lo + HEAD_DIM], place, o_send.at[k], o_recv.at[k], to).start()
            lg[head : head + 1, :] = log_total
        pltpu.make_async_copy(ob.at[k], out_at(k), own_sem.at[k]).start()

    events = []
    for k in range(chunks):
        events.append((CHUNK_STEP * k, 0, k, functools.partial(own, k)))
        for s in range(1, Z):
            events.append((CHUNK_STEP * k + STAGE_STEP * s, 1, k, functools.partial(stage, k, s)))
        last = CHUNK_STEP * k + STAGE_STEP * (Z - 1)
        events.append((last + 2, 2, k, functools.partial(crossed, k)))
        events.append((last + 3, 3, k, functools.partial(compute, k)))
    for event in sorted(events, key=lambda e: e[:3]):
        event[3]()

    log_copy = [copy(lg, log_ref.at[o], l_send, l_recv, to) for to in peers]
    for one in log_copy:
        one.start()
    log_own = pltpu.make_async_copy(lg, log_ref.at[o], l_own)
    log_own.start()

    for k in range(chunks):
        sent = G.at[k, pl.ds(0, (n - 1) * rows), :]
        copy(sent, sent, x_send.at[k], x_recv.at[k], peers[0]).wait_send()
        for s in range(Z - 1):
            @pl.when(jnp.logical_and(has_up, z - s >= 0))
            def _():
                up_copy(k, s).wait_send()

            @pl.when(jnp.logical_and(has_down, z + s < Z))
            def _():
                down_copy(k, s).wait_send()

        b = line(k, y, c)
        copy(b, b, y_send.at[k], y_recv.at[k], across).wait_send()
        sibling_copy(k, y, 0).wait_send()
        sibling_copy(k, 1 - y, 1).wait_send()
        pltpu.make_async_copy(ob.at[k], out_at(k), own_sem.at[k]).wait()
        some = out_ref.at[:, pl.ds(0, (n - 1) * cw)]
        whole = copy(some, some, o_send.at[k], o_recv.at[k], peers[0])
        whole.wait_send()
        whole.wait_recv()
    log_own.wait()
    some = log_ref.at[pl.ds(0, n - 1)]
    whole = copy(some, some, l_send, l_recv, peers[0])
    whole.wait_send()
    whole.wait_recv()


def on_device(n, inner, queries, mem_keys, mem_values):
    tokens, columns = queries.shape
    rows = mem_keys.shape[0]
    Z = inner // 4
    heads = columns // HEAD_DIM
    lh = heads // n
    lc = lh * HEAD_DIM
    cw = math.gcd(lh, CHUNK_HEADS) * HEAD_DIM
    chunks = lc // cw
    R = rows * n
    entries = inner * R
    dma = pltpu.SemaphoreType.DMA
    attended, logs = pl.pallas_call(
        functools.partial(kernel, n, Z, chunks, cw),
        out_shape=(
            jax.ShapeDtypeStruct((tokens, columns), jnp.bfloat16),
            jax.ShapeDtypeStruct((n, lh, tokens), jnp.float32),
        ),
        in_specs=[
            pl.BlockSpec(memory_space=pltpu.HBM),
            pl.BlockSpec(memory_space=pltpu.HBM),
            pl.BlockSpec(memory_space=pltpu.HBM),
        ],
        out_specs=(pl.BlockSpec(memory_space=pl.ANY), pl.BlockSpec(memory_space=pl.ANY)),
        scratch_shapes=[
            pltpu.VMEM(mem_keys.shape, jnp.bfloat16),
            pltpu.VMEM(mem_keys.shape, jnp.bfloat16),
            dma,
            dma,
            pltpu.VMEM((tokens, lc), jnp.bfloat16),
            pltpu.VMEM((n, chunks, rows, 2 * cw), jnp.bfloat16),
            pltpu.VMEM((chunks, entries, 2 * cw), jnp.bfloat16),
            pltpu.VMEM((chunks, tokens, cw), jnp.bfloat16),
            pltpu.VMEM((lh, tokens), jnp.float32),
            dma,
            dma((chunks,)), dma((chunks,)),
            dma((chunks, Z)), dma((chunks, Z)), dma((chunks, Z)), dma((chunks, Z)),
            dma((chunks,)), dma((chunks,)),
            dma((chunks, 2)), dma((chunks, 2)),
            dma((chunks,)), dma((chunks,)), dma((chunks,)),
            dma, dma, dma,
        ],
        compiler_params=pltpu.CompilerParams(
            collective_id=0, has_side_effects=True, vmem_limit_bytes=40 * 2**20
        ),
        cost_estimate=pl.CostEstimate(
            flops=4 * tokens * entries * lc,
            bytes_accessed=4 * tokens * columns,
            transcendentals=tokens * entries * lh,
        ),
    )(queries, mem_keys, mem_values)
    return attended, logs.reshape(heads, tokens).T


def solution(mesh):
    in_specs = (P("inner", None), P(("outer", "inner"), None), P(("outer", "inner"), None))
    out_specs = (P("inner", None), P("inner", None))
    return jax.shard_map(
        functools.partial(on_device, mesh.shape["outer"], mesh.shape["inner"]),
        mesh=mesh, in_specs=in_specs, out_specs=out_specs, check_vma=False,
    )
```
